256 devices in a mesh: cube: 8 (over z), row: 4 (over y_lo, core), col: 8 (over y_hi, x).
Axes of the slice: x: 4, y: 4 (y_hi: 2, y_lo: 2; y = y_hi * 2 + y_lo), z: 8, core: 2. Of those that a mesh axis runs over, the one named last changes fastest.
Arguments:
- diag_block: float32 [8, 256, 256], P('cube', ('row', 'col'))
- pivot_order: int32 [8, 256], P('cube'), may hold values from 0 to 255, as said below
- lower_in: bfloat16 [8, 4096, 256], P('cube', 'row', 'col'), may hold values from -0.14941406 to 0.14941406
- upper_in: bfloat16 [8, 256, 30720], P('cube', 'row', 'col'), may hold values from -6 to 6
- trailing: bfloat16 [8, 4096, 30720], P('cube', 'row', 'col'), may hold values from -6 to 6
- block_mask: int32 [8, 32, 16], P('cube', 'row', 'col'), may hold values 0 or 1
- row_map: int32 [8, 4096], P('cube', 'row'), may hold values from 0 to 1023, as said below
Outputs:
- merged: bfloat16 [8, 4096, 15360], P('cube', 'row', 'col')
The draws below stay inside these ranges and needn't reach their ends.
Inputs may be any that keep to these rules, and one draw needn't show every extreme that they name: `pivot_order`: each front's row is a permutation of 0 to 255. `row_map`: in each aligned block of 1024 rows of a front the entries are a permutation of 0 to 1023.
All inputs are finite; a program needn't handle non-finite values. No bound on the sum of `block_mask` on one device may be relied on, other than what follows from the above.
Results may differ from the reference program's by a relative error of at most 0.0056.
Values may be sent and summed in bfloat16 or wider, within the bound.
A program may use at most 192 MiB of HBM per device.

```python
import jax
import jax.numpy as jnp
from jax import lax

NB = 256
NF = 30720
M_DEV = 1024
BR = 128
FRONTS = 8
M = 4096
N_COL = 8


def pivot_helper(key):
    keys = jax.random.split(jax.random.fold_in(key, 11), FRONTS)
    return jax.vmap(lambda single: jax.random.permutation(single, NB))(keys).astype(jnp.int32)


def draw_pivot_order(key, part):
    return pivot_helper(key)


def draw_diag_block(key, part):
    order = pivot_helper(key)
    lower_key = jax.random.fold_in(key, 23)
    upper_key = jax.random.fold_in(key, 31)
    diag_key = jax.random.fold_in(key, 37)
    shape = (FRONTS, NB, NB)
    lower_ints = jax.random.randint(jax.random.fold_in(lower_key, 1), shape, -4, 5, dtype=jnp.int32) + jax.random.randint(jax.random.fold_in(lower_key, 2), shape, -4, 5, dtype=jnp.int32)
    upper_ints = jax.random.randint(jax.random.fold_in(upper_key, 1), shape, -4, 5, dtype=jnp.int32) + jax.random.randint(jax.random.fold_in(upper_key, 2), shape, -4, 5, dtype=jnp.int32)
    diag_ints = jax.random.randint(diag_key, (FRONTS, NB), 24, 175, dtype=jnp.int32)
    rows = jnp.arange(NB, dtype=jnp.int32)[:, None]
    cols = jnp.arange(NB, dtype=jnp.int32)[None, :]
    below = (rows > cols).astype(jnp.int32)
    above = (rows < cols).astype(jnp.int32)
    ident = (rows == cols).astype(jnp.int32)
    unit_lower = lower_ints * below[None] + 64 * ident[None]
    upper_tri = upper_ints * above[None] + diag_ints[:, :, None] * ident[None]
    product = jnp.matmul(unit_lower, upper_tri)
    base = product.astype(jnp.float32) / 4096.0
    return jax.vmap(lambda block_rows, perm: jnp.zeros((NB, NB), jnp.float32).at[perm].set(block_rows))(base, order)


def draw_row_map(key, part):
    count = FRONTS * (M // M_DEV)
    keys = jax.random.split(jax.random.fold_in(key, 5), count)
    perms = jax.vmap(lambda single: jax.random.permutation(single, M_DEV))(keys)
    return perms.reshape(FRONTS, M).astype(jnp.int32)


def place_ends(entries, stream_key, least, top_value):
    longest = entries.shape.index(max(entries.shape))
    spots = []
    for shift in (0, 1):
        where = [jax.random.randint(jax.random.fold_in(stream_key, axis), (), 0, length) for axis, length in enumerate(entries.shape)]
        where[longest] = (where[longest] + shift) % entries.shape[longest]
        spots.append(tuple(where))
    return entries.at[spots[0]].set(least).at[spots[1]].set(top_value)


def levels(own_key, dims, cuts, low, high):
    factor_of, own = 1.0, jax.random.fold_in(own_key, 6)
    for position, parts in cuts:
        steps = jnp.exp(jax.random.uniform(jax.random.fold_in(own, position), (parts,), jnp.float32, low / len(cuts), high / len(cuts)))
        factor_of = factor_of * jnp.repeat(steps, dims[position] // parts).reshape([-1 if axis == position else 1 for axis in range(len(dims))])
    return factor_of


def gaussian(rng, dims, scale, limit, cuts=(), held_as=jnp.bfloat16):
    result = jax.random.normal(rng, dims, jnp.float32) * scale
    if len(cuts) > 0:
        result = levels(rng, dims, cuts, -0.22, 0.18) * result
    return jnp.clip(result, min=-limit, max=limit).astype(held_as)


def setup_inputs(seed: int = 0) -> dict:
    splits = jax.random.split(jax.random.key(seed), 8)
    return {
        "diag_block": draw_diag_block(jax.random.fold_in(splits[7], 71), 0),
        "pivot_order": draw_pivot_order(jax.random.fold_in(splits[7], 71), 0),
        "lower_in": gaussian(splits[2], (FRONTS, M, NB), 0.025, 0.14941406, ((0, 8), (1, 4), (2, 8))),
        "upper_in": gaussian(splits[3], (FRONTS, NB, NF), 1.0, 6.0, ((0, 8), (1, 4), (2, 8))),
        "trailing": gaussian(splits[4], (FRONTS, M, NF), 1.0, 6.0, ((0, 8), (1, 4), (2, 8))),
        "block_mask": place_ends((jax.random.randint(splits[5], (FRONTS, M // BR, 2 * N_COL), 0, 4) < 3).astype(jnp.int32), jax.random.fold_in(splits[5], 1), 0, 1),
        "row_map": draw_row_map(jax.random.fold_in(splits[7], 71), 0),
    }


def exact_product(left, right):
    return jnp.dot(left, right, precision=lax.Precision.HIGHEST, preferred_element_type=left.dtype)


def small_inverses(block):
    size = block.shape[0]
    work = block
    for step in range(size - 1):
        column = work[step + 1:, step] / work[step, step]
        work = work.at[step + 1:, step + 1:].add(-column[:, None] * work[step, step + 1:][None, :])
        work = work.at[step + 1:, step].set(column)
    identity = jnp.eye(size, dtype=block.dtype)
    lower = jnp.tril(work, -1) + identity
    upper = jnp.triu(work)
    lower_rows = []
    for step in range(size):
        fresh = identity[step]
        for inner in range(step):
            fresh = fresh - lower[step, inner] * lower_rows[inner]
        lower_rows.append(fresh)
    upper_rows = [None] * size
    for step in range(size - 1, -1, -1):
        fresh = identity[step]
        for inner in range(step + 1, size):
            fresh = fresh - upper[step, inner] * upper_rows[inner]
        upper_rows[step] = fresh / upper[step, step]
    return jnp.stack(lower_rows), jnp.stack(upper_rows)


def block_inverses(block):
    size = block.shape[0]
    if size <= 8:
        return small_inverses(block)
    half = size // 2
    lower_one, upper_one = block_inverses(block[:half, :half])
    lower_side = exact_product(block[half:, :half], upper_one)
    upper_side = exact_product(lower_one, block[:half, half:])
    schur = block[half:, half:] - exact_product(lower_side, upper_side)
    lower_two, upper_two = block_inverses(schur)
    zero = jnp.zeros((half, half), block.dtype)
    corner_lower = -exact_product(lower_two, exact_product(lower_side, lower_one))
    corner_upper = -exact_product(upper_one, exact_product(upper_side, upper_two))
    lower_inv = jnp.concatenate([jnp.concatenate([lower_one, zero], axis=1), jnp.concatenate([corner_lower, lower_two], axis=1)], axis=0)
    upper_inv = jnp.concatenate([jnp.concatenate([upper_one, corner_upper], axis=1), jnp.concatenate([zero, upper_two], axis=1)], axis=0)
    return lower_inv, upper_inv


def front_update(diag, order, below_panel, right_panel, block, mask):
    lower_inv, upper_inv = block_inverses(jnp.take(diag, order, axis=0))
    lower_panel = jnp.dot(below_panel.astype(jnp.float32), upper_inv, precision=lax.Precision.HIGHEST, preferred_element_type=jnp.float32).astype(jnp.bfloat16)
    upper_panel = jnp.dot(lower_inv, jnp.take(right_panel, order, axis=0).astype(jnp.float32), precision=lax.Precision.HIGHEST, preferred_element_type=jnp.float32).astype(jnp.bfloat16)
    product = jnp.dot(lower_panel, upper_panel, preferred_element_type=jnp.float32)
    blocks, tiles = mask.shape
    masked = (product.reshape(blocks, -1, tiles, product.shape[1] // tiles) * mask.astype(jnp.float32)[:, None, :, None]).reshape(product.shape)
    return (block.astype(jnp.float32) - masked).astype(jnp.bfloat16)


def extend_add(mine, other, mapping, side):
    width = NF // (2 * N_COL)
    kept = mine.reshape(M, N_COL, 2, width)[:, :, side, :]
    starts = (jnp.arange(M, dtype=jnp.int32) // M_DEV) * M_DEV
    source = (starts + mapping).astype(jnp.int32)
    taken = jnp.take(other.reshape(M, N_COL, 2, width), source, axis=0)[:, :, side, :]
    return (kept.astype(jnp.float32) + taken.astype(jnp.float32)).astype(jnp.bfloat16).reshape(M, NF // 2)


def reference(diag_block, pivot_order, lower_in, upper_in, trailing, block_mask, row_map):
    pairs = FRONTS // 2

    def per_pair(items):
        diag, order, below_panel, right_panel, block, mask, mapping = items
        first = front_update(diag[0], order[0], below_panel[0], right_panel[0], block[0], mask[0])
        second = front_update(diag[1], order[1], below_panel[1], right_panel[1], block[1], mask[1])
        return (extend_add(first, second, mapping[0], 0), extend_add(second, first, mapping[1], 1))

    inputs = (diag_block, pivot_order, lower_in, upper_in, trailing, block_mask, row_map)
    stacked = tuple(item.reshape((pairs, 2) + item.shape[1:]) for item in inputs)
    even_out, odd_out = lax.map(per_pair, stacked)
    return jnp.stack([even_out, odd_out], axis=1).reshape(FRONTS, M, NF // 2)
```

```python
import functools

import jax
import jax.numpy as jnp
from jax import lax
from jax.experimental import pallas as pl
from jax.experimental.pallas import tpu as pltpu
from jax.sharding import PartitionSpec as P

MESH = pl.DeviceIdType.MESH
RAW = (384, 384, 384)
COOKED = (384, 256, 128)
STEP = 64


def offsets(widths, start):
    spans = []
    for width in widths:
        spans.append((start, width))
        start += width
    return spans


def invert(amat):
    size = amat.shape[0]
    lane = lax.broadcasted_iota(jnp.int32, (1, size), 1)
    sub = lax.broadcasted_iota(jnp.int32, (STEP, 1), 0)

    def block_step(_, carry):
        x = amat[0:STEP, :]
        for k in range(STEP):
            column = jnp.broadcast_to(x[:, k : k + 1], (STEP, size))
            here = lane == k
            inverse = 1.0 / column[k : k + 1, :]
            fresh = jnp.where(here, inverse, x[k : k + 1, :] * inverse)
            x = jnp.where(sub == k, fresh, jnp.where(here, 0.0, x) - column * fresh)
        below = amat[STEP:, :]
        rest = jnp.where(lane < STEP, 0.0, below) - jnp.dot(
            below[:, 0:STEP],
            x,
            precision=lax.Precision.HIGHEST,
            preferred_element_type=jnp.float32,
        )
        amat[0 : size - STEP, :] = jnp.concatenate([rest[:, STEP:], rest[:, :STEP]], axis=1)
        amat[size - STEP :, :] = jnp.concatenate([x[:, STEP:], x[:, :STEP]], axis=1)
        return carry

    lax.fori_loop(0, size // STEP, block_step, 0)


def update(block, spans_from, panel, right, right_from, width):
    rows = 256

    def body(step, carry):
        top = pl.multiple_of(step * rows, rows)
        product = jnp.dot(
            panel[pl.ds(top, rows), :],
            right[:, pl.ds(right_from, width)],
            preferred_element_type=jnp.float32,
        )
        where = (pl.ds(top, rows), pl.ds(spans_from, width))
        block[where] = (block[where].astype(jnp.float32) - product).astype(jnp.bfloat16)
        return carry

    lax.fori_loop(0, block.shape[0] // rows, body, 0)


def kernel(
    diag, order_s, order_v, lower, upper, trailing, mask, row_map, out,
    dg, lt, u, ug, land, keep, cook, amat, wk, ws, wo, wg, mo, mg, perm,
    d_send, d_recv, l_send, l_recv, u_send, u_recv, f_send, f_recv,
    v_send, v_recv, z_send, z_recv, local_sem, out_sem,
):
    n_row, n_col = lax.axis_size("row"), lax.axis_size("col")
    c, r, q = lax.axis_index("cube"), lax.axis_index("row"), lax.axis_index("col")
    parity = lax.rem(c, 2)
    peer = (c + 1 - 2 * parity, r, q)
    row_mates = [(c, lax.rem(r + d, n_row), q) for d in range(1, n_row)]
    col_mates = [(c, r, lax.rem(q + d, n_col)) for d in range(1, n_col)]

    m_dev = keep.shape[0]
    half = keep.shape[1]
    raw_width = ug.shape[1]
    kept_at = pl.multiple_of(parity * half, 128)
    sent_at = pl.multiple_of((1 - parity) * half, 128)
    raw_spans = offsets(RAW, 0)
    cooked_spans = offsets(COOKED, raw_width)

    def remote(src, dst, send, recv, to):
        return pltpu.make_async_remote_copy(
            src_ref=src, dst_ref=dst, send_sem=send, recv_sem=recv,
            device_id=to, device_id_type=MESH,
        )

    barrier = pltpu.get_barrier_semaphore()
    for mate in [peer] + row_mates + col_mates:
        pl.semaphore_signal(barrier, inc=1, device_id=mate, device_id_type=MESH)
    pl.semaphore_wait(barrier, n_row + n_col - 1)

    d_rows = diag.shape[1]
    d_at = pl.multiple_of(q * d_rows, d_rows)
    u_rows = upper.shape[1]
    u_at = pl.multiple_of(r * u_rows, u_rows)
    l_rows = lower.shape[1]
    l_at = pl.multiple_of(q * l_rows, l_rows)
    w_rows = m_dev // n_col
    w_at = pl.multiple_of(q * w_rows, w_rows)

    d_own = pltpu.make_async_copy(diag.at[0], dg.at[r, pl.ds(d_at, d_rows), :], local_sem.at[0])
    d_own.start()
    d_first = []
    for i, mate in enumerate(row_mates):
        copy = remote(diag.at[0], dg.at[r, pl.ds(d_at, d_rows), :], d_send.at[i], d_recv.at[i], mate)
        copy.start()
        d_first.append(copy)

    for i in range(mo.shape[0]):
        flag = mask[0, 1 - parity, i].astype(jnp.float32)
        mo[i : i + 1, :] = jnp.full((1, mo.shape[1]), flag, jnp.float32)
    z_copies = []

    def to_peer(src, dst):
        i = len(z_copies)
        copy = remote(src, dst, z_send.at[i], z_recv.at[i], peer)
        copy.start()
        z_copies.append(copy)
        return copy

    m_raw = to_peer(mo, mg)
    u_raw = to_peer(
        upper.at[0, :, pl.ds(sent_at, raw_width)], ug.at[pl.ds(u_at, u_rows), :]
    )
    raw = [
        to_peer(trailing.at[0, :, pl.ds(sent_at + at, width)], land.at[:, pl.ds(at, width)])
        for at, width in raw_spans
    ]

    d_own.wait()
    for copy in d_first:
        copy.wait_recv()
    d_second = []
    for i, mate in enumerate(col_mates):
        part = dg.at[:, pl.ds(d_at, d_rows), :]
        copy = remote(part, part, d_send.at[n_row - 1 + i], d_recv.at[n_row - 1 + i], mate)
        copy.start()
        d_second.append(copy)

    l_own = pltpu.make_async_copy(lower.at[0], lt.at[pl.ds(l_at, l_rows), :], local_sem.at[1])
    l_own.start()
    l_copies = []
    for i, mate in enumerate(col_mates):
        copy = remote(lower.at[0], lt.at[pl.ds(l_at, l_rows), :], l_send.at[i], l_recv.at[i], mate)
        copy.start()
        l_copies.append(copy)
    u_own = pltpu.make_async_copy(upper.at[0], u.at[pl.ds(u_at, u_rows), :], local_sem.at[2])
    u_own.start()
    u_copies = []
    for i, mate in enumerate(row_mates):
        copy = remote(upper.at[0], u.at[pl.ds(u_at, u_rows), :], u_send.at[i], u_recv.at[i], mate)
        copy.start()
        u_copies.append(copy)
    cook_in = pltpu.make_async_copy(
        trailing.at[0, :, pl.ds(sent_at + raw_width, half - raw_width)], cook, local_sem.at[3]
    )
    cook_in.start()
    keep_in = pltpu.make_async_copy(
        trailing.at[0, :, pl.ds(kept_at, half)], keep, local_sem.at[4]
    )
    keep_in.start()

    tile = 128
    lane = lax.broadcasted_iota(jnp.int32, (tile, tile), 1)
    for i in range(m_dev // tile):
        along = jnp.broadcast_to(row_map[:, i * tile : (i + 1) * tile], (tile, tile))
        target = along.astype(jnp.float32).T.astype(jnp.int32)
        for j in range(m_dev // tile):
            hit = jnp.where(lane + j * tile == target, 1.0, 0.0)
            perm[i * tile : (i + 1) * tile, j * tile : (j + 1) * tile] = hit.astype(jnp.bfloat16)

    for copy in d_second:
        copy.wait_recv()
    size = amat.shape[0]
    per_row = dg.shape[1]

    def pick(i, carry):
        source = order_s[0, i]
        amat[pl.ds(i, 1), :] = dg[source // per_row, pl.ds(source % per_row, 1), :]
        return carry

    lax.fori_loop(0, size, pick, 0)
    invert(amat)

    u_raw.wait_recv()
    u_pass = []
    for i, mate in enumerate(row_mates):
        part = ug.at[pl.ds(u_at, u_rows), :]
        copy = remote(part, part, f_send.at[i], f_recv.at[i], mate)
        copy.start()
        u_pass.append(copy)

    xt = amat[...].T
    high = xt.astype(jnp.bfloat16)
    left = xt - high.astype(jnp.float32)
    middle = left.astype(jnp.bfloat16)
    low = (left - middle.astype(jnp.float32)).astype(jnp.bfloat16)
    subs = lax.broadcasted_iota(jnp.int32, (size, size), 0)
    hot = jnp.where(subs == order_v[...], 1.0, 0.0).astype(jnp.bfloat16)
    l_own.wait()
    for copy in l_copies:
        copy.wait_recv()

    def panel(i, carry):
        at = pl.multiple_of(i * tile, tile)
        part = lt[:, pl.ds(at, tile)]
        wt = (
            jnp.dot(low, part, preferred_element_type=jnp.float32)
            + jnp.dot(middle, part, preferred_element_type=jnp.float32)
            + jnp.dot(high, part, preferred_element_type=jnp.float32)
        )
        w = jnp.dot(hot, wt.astype(jnp.bfloat16), preferred_element_type=jnp.float32).T
        wk[pl.ds(at, tile), :] = (w * mask[0, parity, i].astype(jnp.float32)).astype(jnp.bfloat16)
        ws[pl.ds(at, tile), :] = (w * mask[0, 1 - parity, i].astype(jnp.float32)).astype(jnp.bfloat16)
        wo[pl.ds(at, tile), :] = w.astype(jnp.bfloat16)
        return carry

    lax.fori_loop(0, m_dev // tile, panel, 0)
    w_raw = to_peer(wo.at[pl.ds(w_at, w_rows), :], wg.at[pl.ds(w_at, w_rows), :])

    u_own.wait()
    for copy in u_copies:
        copy.wait_recv()
    cook_in.wait()
    cooked = []
    for at, width in cooked_spans:
        start = at - raw_width
        update(cook, start, ws, u, sent_at + at, width)
        cooked.append(to_peer(cook.at[:, pl.ds(start, width)], land.at[:, pl.ds(at, width)]))

    keep_in.wait()
    for at in range(0, half, 384):
        update(keep, at, wk, u, kept_at + at, 384)

    w_raw.wait_recv()
    w_pass = []
    for i, mate in enumerate(col_mates):
        part = wg.at[pl.ds(w_at, w_rows), :]
        copy = remote(part, part, v_send.at[i], v_recv.at[i], mate)
        copy.start()
        w_pass.append(copy)
    for copy in [m_raw] + u_pass + w_pass:
        copy.wait_recv()
    for i in range(mg.shape[0]):
        block = slice(i * tile, (i + 1) * tile)
        masked = wg[block, :].astype(jnp.float32) * mg[i : i + 1, :]
        ws[block, :] = masked.astype(jnp.bfloat16)

    def merge(at, width):
        rows = 256

        def body(step, carry):
            top = pl.multiple_of(step * rows, rows)
            taken = jnp.dot(
                perm[pl.ds(top, rows), :],
                land[:, at : at + width],
                preferred_element_type=jnp.float32,
            )
            where = (pl.ds(top, rows), pl.ds(at, width))
            keep[where] = (keep[where].astype(jnp.float32) + taken).astype(jnp.bfloat16)
            return carry

        lax.fori_loop(0, m_dev // rows, body, 0)

    outs = []

    def write(at, width):
        i = len(outs)
        copy = pltpu.make_async_copy(
            keep.at[:, pl.ds(at, width)], out.at[0, :, pl.ds(at, width)], out_sem.at[i]
        )
        copy.start()
        outs.append(copy)

    for (at, width), copy in zip(raw_spans, raw):
        copy.wait_recv()
        update(land, at, ws, ug, at, width)
        merge(at, width)
        write(at, width)
    for (at, width), copy in zip(cooked_spans, cooked):
        copy.wait_recv()
        merge(at, width)
        write(at, width)

    for copy in d_first + d_second + l_copies + u_copies + u_pass + w_pass + z_copies:
        copy.wait_send()
    for copy in outs:
        copy.wait()


def local(diag_block, pivot_order, lower_in, upper_in, trailing, block_mask, row_map):
    n_row, n_col = lax.axis_size("row"), lax.axis_size("col")
    size = diag_block.shape[2]
    m_dev, wide = trailing.shape[1:]
    half = wide // 2
    raw_width = sum(RAW)
    n_z = 3 + len(RAW) + len(COOKED)
    dma = pltpu.SemaphoreType.DMA
    bf16, f32 = jnp.bfloat16, jnp.float32
    hbm = pl.BlockSpec(memory_space=pl.ANY)
    vmem = pl.BlockSpec(memory_space=pltpu.VMEM)
    smem = pl.BlockSpec(memory_space=pltpu.SMEM)
    return pl.pallas_call(
        kernel,
        out_shape=jax.ShapeDtypeStruct((1, m_dev, half), bf16),
        in_specs=[hbm, smem, vmem, hbm, hbm, hbm, smem, vmem],
        out_specs=hbm,
        scratch_shapes=[
            pltpu.VMEM((n_row, size // n_row, size), f32),
            pltpu.VMEM((size, m_dev), bf16),
            pltpu.VMEM((size, wide), bf16),
            pltpu.VMEM((size, raw_width), bf16),
            pltpu.VMEM((m_dev, half), bf16),
            pltpu.VMEM((m_dev, half), bf16),
            pltpu.VMEM((m_dev, half - raw_width), bf16),
            pltpu.VMEM((size, size), f32),
            pltpu.VMEM((m_dev, size), bf16),
            pltpu.VMEM((m_dev, size), bf16),
            pltpu.VMEM((m_dev, size), bf16),
            pltpu.VMEM((m_dev, size), bf16),
            pltpu.VMEM((block_mask.shape[1], size), f32),
            pltpu.VMEM((block_mask.shape[1], size), f32),
            pltpu.VMEM((m_dev, m_dev), bf16),
            dma((n_row + n_col - 2,)), dma((n_row + n_col - 2,)),
            dma((n_col - 1,)), dma((n_col - 1,)),
            dma((n_row - 1,)), dma((n_row - 1,)),
            dma((n_row - 1,)), dma((n_row - 1,)),
            dma((n_col - 1,)), dma((n_col - 1,)),
            dma((n_z,)), dma((n_z,)),
            dma((5,)),
            dma((len(RAW) + len(COOKED),)),
        ],
        compiler_params=pltpu.CompilerParams(
            collective_id=0, has_side_effects=True, vmem_limit_bytes=48 * 1024 * 1024
        ),
    )(
        diag_block,
        pivot_order,
        pivot_order,
        jnp.swapaxes(lower_in, 1, 2),
        upper_in,
        trailing,
        jnp.swapaxes(block_mask, 1, 2),
        row_map,
    )


def solution(mesh):
    return jax.shard_map(
        local,
        mesh=mesh,
        in_specs=(
            P("cube", ("row", "col"), None),
            P("cube", None),
            P("cube", "row", "col"),
            P("cube", "row", "col"),
            P("cube", "row", "col"),
            P("cube", "row", "col"),
            P("cube", "row"),
        ),
        out_specs=P("cube", "row", "col"),
        check_vma=False,
    )
```

```python
import functools

import jax
import jax.numpy as jnp
from jax import lax
from jax.experimental import pallas as pl
from jax.experimental.pallas import tpu as pltpu
from jax.sharding import PartitionSpec as P

MESH = pl.DeviceIdType.MESH
RAW = (512, 384)
COOKED = (128, 256, 256, 256, 128)
STEP = 64
GROUP = 8


def offsets(widths, start):
    spans = []
    for width in widths:
        spans.append((start, width))
        start += width
    return spans


def invert(amat):
    size = amat.shape[0]
    narrow = 128
    lane = lax.broadcasted_iota(jnp.int32, (1, size), 1)
    sub = lax.broadcasted_iota(jnp.int32, (STEP, 1), 0)

    def block_step(_, carry):
        x = amat[0:STEP, :]
        for first in range(0, STEP, GROUP):
            columns = [
                jnp.broadcast_to(x[:, k : k + 1], (STEP, narrow))
                for k in range(first, first + GROUP)
            ]
            for j in range(GROUP):
                k = first + j
                inverse = 1.0 / columns[j][k : k + 1, :]
                for later in range(j + 1, GROUP):
                    ratio = columns[later][k : k + 1, :] * inverse
                    columns[later] = jnp.where(
                        sub == k, ratio, columns[later] - columns[j] * ratio
                    )
                here = lane == k
                column = jnp.concatenate([columns[j]] * (size // narrow), axis=1)
                inverse = jnp.concatenate([inverse] * (size // narrow), axis=1)
                fresh = jnp.where(here, inverse, x[k : k + 1, :] * inverse)
                x = jnp.where(sub == k, fresh, jnp.where(here, 0.0, x) - column * fresh)
        below = amat[STEP:, :]
        rest = jnp.where(lane < STEP, 0.0, below) - jnp.dot(
            below[:, 0:STEP],
            x,
            precision=lax.Precision.HIGHEST,
            preferred_element_type=jnp.float32,
        )
        amat[0 : size - STEP, :] = jnp.concatenate([rest[:, STEP:], rest[:, :STEP]], axis=1)
        amat[size - STEP :, :] = jnp.concatenate([x[:, STEP:], x[:, :STEP]], axis=1)
        return carry

    lax.fori_loop(0, size // STEP, block_step, 0)


def update(block, spans_from, panel, right, right_from, width):
    rows = 256

    def body(step, carry):
        top = pl.multiple_of(step * rows, rows)
        product = jnp.dot(
            panel[pl.ds(top, rows), :],
            right[:, pl.ds(right_from, width)],
            preferred_element_type=jnp.float32,
        )
        where = (pl.ds(top, rows), pl.ds(spans_from, width))
        block[where] = (block[where].astype(jnp.float32) - product).astype(jnp.bfloat16)
        return carry

    lax.fori_loop(0, block.shape[0] // rows, body, 0)


def kernel(
    diag, order_in, lower, upper, trailing, mask_in, row_map_in, keep,
    order_s, order_v, mask, row_map, dg, lt, u, ug, land, cook, amat, wk, ws, wo, wg, mo, mg, perm,
    d_send, d_recv, l_send, l_recv, u_send, u_recv, f_send, f_recv,
    v_send, v_recv, z_send, z_recv, local_sem, gate,
):
    n_row, n_col = lax.axis_size("row"), lax.axis_size("col")
    c, r, q = lax.axis_index("cube"), lax.axis_index("row"), lax.axis_index("col")
    parity = lax.rem(c, 2)
    peer = (c + 1 - 2 * parity, r, q)
    row_mates = [(c, lax.rem(r + d, n_row), q) for d in range(1, n_row)]
    col_mates = [(c, r, lax.rem(q + d, n_col)) for d in range(1, n_col)]

    m_dev = keep.shape[0]
    half = keep.shape[1]
    raw_width = ug.shape[1]
    kept_at = pl.multiple_of(parity * half, 128)
    sent_at = pl.multiple_of((1 - parity) * half, 128)
    raw_spans = offsets(RAW, 0)
    cooked_spans = offsets(COOKED, raw_width)

    def remote(src, dst, send, recv, to):
        return pltpu.make_async_remote_copy(
            src_ref=src, dst_ref=dst, send_sem=send, recv_sem=recv,
            device_id=to, device_id_type=MESH,
        )

    small = []
    for i, (src, dst) in enumerate(
        [(mask_in, mask), (order_in, order_s), (order_in, order_v), (row_map_in, row_map)]
    ):
        copy = pltpu.make_async_copy(src, dst, local_sem.at[5 + i])
        copy.start()
        small.append(copy)

    barrier = pltpu.get_barrier_semaphore()

    def signal(semaphore, to):
        pl.semaphore_signal(semaphore, inc=1, device_id=to, device_id_type=MESH)

    @pl.when(parity == 1)
    def _():
        signal(barrier, peer)

    @pl.when(parity == 0)
    def _():
        pl.semaphore_wait(barrier, 1)
        signal(gate, peer)

    @pl.when(parity == 1)
    def _():
        pl.semaphore_wait(gate, 1)

    d_rows = diag.shape[1]
    d_at = pl.multiple_of(q * d_rows, d_rows)
    u_rows = upper.shape[1]
    u_at = pl.multiple_of(r * u_rows, u_rows)
    l_rows = lower.shape[1]
    l_at = pl.multiple_of(q * l_rows, l_rows)
    w_rows = m_dev // n_col
    w_at = pl.multiple_of(q * w_rows, w_rows)

    z_copies = []

    def to_peer(src, dst):
        i = len(z_copies)
        copy = remote(src, dst, z_send.at[i], z_recv.at[i], peer)
        copy.start()
        z_copies.append(copy)
        return copy

    raw = [
        to_peer(trailing.at[0, :, pl.ds(sent_at + at, width)], land.at[:, pl.ds(at, width)])
        for at, width in raw_spans
    ]
    u_raw = to_peer(
        upper.at[0, :, pl.ds(sent_at, raw_width)], ug.at[pl.ds(u_at, u_rows), :]
    )

    @pl.when(parity == 1)
    def _():
        for mate in row_mates + col_mates:
            signal(barrier, mate)
        pl.semaphore_wait(barrier, n_row + n_col - 2)
        signal(gate, peer)

    @pl.when(parity == 0)
    def _():
        pl.semaphore_wait(gate, 1)

    d_own = pltpu.make_async_copy(diag.at[0], dg.at[r, pl.ds(d_at, d_rows), :], local_sem.at[0])
    d_own.start()
    d_first = []
    for i, mate in enumerate(row_mates):
        copy = remote(diag.at[0], dg.at[r, pl.ds(d_at, d_rows), :], d_send.at[i], d_recv.at[i], mate)
        copy.start()
        d_first.append(copy)

    small[0].wait()
    for i in range(mo.shape[0]):
        flag = mask[0, 1 - parity, i].astype(jnp.float32)
        mo[i : i + 1, :] = jnp.full((1, mo.shape[1]), flag, jnp.float32)
    m_raw = to_peer(mo, mg)

    d_own.wait()
    for copy in d_first:
        copy.wait_recv()
    d_second = []
    for i, mate in enumerate(col_mates):
        part = dg.at[:, pl.ds(d_at, d_rows), :]
        copy = remote(part, part, d_send.at[n_row - 1 + i], d_recv.at[n_row - 1 + i], mate)
        copy.start()
        d_second.append(copy)

    l_own = pltpu.make_async_copy(lower.at[0], lt.at[pl.ds(l_at, l_rows), :], local_sem.at[1])
    l_own.start()
    l_copies = []
    for i, mate in enumerate(col_mates):
        copy = remote(lower.at[0], lt.at[pl.ds(l_at, l_rows), :], l_send.at[i], l_recv.at[i], mate)
        copy.start()
        l_copies.append(copy)
    u_own = pltpu.make_async_copy(upper.at[0], u.at[pl.ds(u_at, u_rows), :], local_sem.at[2])
    u_own.start()
    u_copies = []
    for i, mate in enumerate(row_mates):
        copy = remote(upper.at[0], u.at[pl.ds(u_at, u_rows), :], u_send.at[i], u_recv.at[i], mate)
        copy.start()
        u_copies.append(copy)
    cook_in = pltpu.make_async_copy(
        trailing.at[0, :, pl.ds(sent_at + raw_width, half - raw_width)], cook, local_sem.at[3]
    )
    cook_in.start()
    keep_in = pltpu.make_async_copy(
        trailing.at[0, :, pl.ds(kept_at, half)], keep, local_sem.at[4]
    )
    keep_in.start()

    for copy in small[1:]:
        copy.wait()
    tile = 128
    lane = lax.broadcasted_iota(jnp.int32, (tile, tile), 1)
    for i in range(m_dev // tile):
        along = jnp.broadcast_to(row_map[:, i * tile : (i + 1) * tile], (tile, tile))
        target = along.astype(jnp.float32).T.astype(jnp.int32)
        for j in range(m_dev // tile):
            hit = jnp.where(lane + j * tile == target, 1.0, 0.0)
            perm[i * tile : (i + 1) * tile, j * tile : (j + 1) * tile] = hit.astype(jnp.bfloat16)

    for copy in d_second:
        copy.wait_recv()
    size = amat.shape[0]
    per_row = dg.shape[1]

    def pick(i, carry):
        source = order_s[0, i]
        amat[pl.ds(i, 1), :] = dg[source // per_row, pl.ds(source % per_row, 1), :]
        return carry

    lax.fori_loop(0, size, pick, 0, unroll=8)
    invert(amat)

    u_raw.wait_recv()
    u_pass = []
    for i, mate in enumerate(row_mates):
        part = ug.at[pl.ds(u_at, u_rows), :]
        copy = remote(part, part, f_send.at[i], f_recv.at[i], mate)
        copy.start()
        u_pass.append(copy)

    xt = amat[...].T
    high = xt.astype(jnp.bfloat16)
    left = xt - high.astype(jnp.float32)
    middle = left.astype(jnp.bfloat16)
    low = (left - middle.astype(jnp.float32)).astype(jnp.bfloat16)
    subs = lax.broadcasted_iota(jnp.int32, (size, size), 0)
    hot = jnp.where(subs == order_v[...], 1.0, 0.0).astype(jnp.bfloat16)
    high, middle, low = [
        jnp.dot(hot, part, preferred_element_type=jnp.float32).astype(jnp.bfloat16)
        for part in (high, middle, low)
    ]
    l_own.wait()
    for copy in l_copies:
        copy.wait_recv()
    wide = 256

    def panel(i, carry):
        part = lt[:, pl.ds(pl.multiple_of(i * wide, wide), wide)]
        wt = (
            jnp.dot(low, part, preferred_element_type=jnp.float32)
            + jnp.dot(middle, part, preferred_element_type=jnp.float32)
            + jnp.dot(high, part, preferred_element_type=jnp.float32)
        )
        w = wt.T
        for j in range(wide // tile):
            at = pl.multiple_of(i * wide + j * tile, tile)
            rows = w[j * tile : (j + 1) * tile, :]
            flag = mask[0, 1 - parity, i * (wide // tile) + j].astype(jnp.float32)
            ws[pl.ds(at, tile), :] = (rows * flag).astype(jnp.bfloat16)
            wo[pl.ds(at, tile), :] = rows.astype(jnp.bfloat16)
        return carry

    lax.fori_loop(0, m_dev // wide, panel, 0)
    w_raw = to_peer(wo.at[pl.ds(w_at, w_rows), :], wg.at[pl.ds(w_at, w_rows), :])

    u_own.wait()
    for copy in u_copies:
        copy.wait_recv()
    cook_in.wait()
    cooked = []
    for at, width in cooked_spans:
        start = at - raw_width
        update(cook, start, ws, u, sent_at + at, width)
        cooked.append(to_peer(cook.at[:, pl.ds(start, width)], land.at[:, pl.ds(at, width)]))

    for i in range(m_dev // tile):
        block = slice(i * tile, (i + 1) * tile)
        flag = mask[0, parity, i].astype(jnp.float32)
        wk[block, :] = (wo[block, :].astype(jnp.float32) * flag).astype(jnp.bfloat16)
    keep_in.wait()
    for at in range(0, half, 384):
        update(keep, at, wk, u, kept_at + at, 384)

    w_raw.wait_recv()
    w_pass = []
    for i, mate in enumerate(col_mates):
        part = wg.at[pl.ds(w_at, w_rows), :]
        copy = remote(part, part, v_send.at[i], v_recv.at[i], mate)
        copy.start()
        w_pass.append(copy)
    for copy in [m_raw] + u_pass + w_pass:
        copy.wait_recv()
    for i in range(mg.shape[0]):
        block = slice(i * tile, (i + 1) * tile)
        masked = wg[block, :].astype(jnp.float32) * mg[i : i + 1, :]
        ws[block, :] = masked.astype(jnp.bfloat16)

    def merge(at, width):
        rows = 512 if width <= tile else 256

        def body(step, carry):
            top = pl.multiple_of(step * rows, rows)
            taken = jnp.dot(
                perm[pl.ds(top, rows), :],
                land[:, at : at + width],
                preferred_element_type=jnp.float32,
            )
            where = (pl.ds(top, rows), pl.ds(at, width))
            keep[where] = (keep[where].astype(jnp.float32) + taken).astype(jnp.bfloat16)
            return carry

        lax.fori_loop(0, m_dev // rows, body, 0)

    for (at, width), copy in zip(raw_spans, raw):
        copy.wait_recv()
        update(land, at, ws, ug, at, width)
        merge(at, width)
    for (at, width), copy in zip(cooked_spans, cooked):
        copy.wait_recv()
        merge(at, width)

    for copy in d_first + d_second + l_copies + u_copies + u_pass + w_pass + z_copies:
        copy.wait_send()


def local(diag_block, pivot_order, lower_in, upper_in, trailing, block_mask, row_map):
    n_row, n_col = lax.axis_size("row"), lax.axis_size("col")
    size = diag_block.shape[2]
    m_dev, wide = trailing.shape[1:]
    half = wide // 2
    raw_width = sum(RAW)
    n_z = 3 + len(RAW) + len(COOKED)
    dma = pltpu.SemaphoreType.DMA
    bf16, f32 = jnp.bfloat16, jnp.float32
    hbm = pl.BlockSpec(memory_space=pltpu.HBM)
    merged = pl.pallas_call(
        kernel,
        out_shape=jax.ShapeDtypeStruct((m_dev, half), bf16),
        in_specs=[hbm] * 7,
        out_specs=pl.BlockSpec(memory_space=pltpu.VMEM),
        scratch_shapes=[
            pltpu.SMEM(pivot_order.shape, jnp.int32),
            pltpu.VMEM(pivot_order.shape, jnp.int32),
            pltpu.SMEM((1, block_mask.shape[2], block_mask.shape[1]), jnp.int32),
            pltpu.VMEM(row_map.shape, jnp.int32),
            pltpu.VMEM((n_row, size // n_row, size), f32),
            pltpu.VMEM((size, m_dev), bf16),
            pltpu.VMEM((size, wide), bf16),
            pltpu.VMEM((size, raw_width), bf16),
            pltpu.VMEM((m_dev, half), bf16),
            pltpu.VMEM((m_dev, half - raw_width), bf16),
            pltpu.VMEM((size, size), f32),
            pltpu.VMEM((m_dev, size), bf16),
            pltpu.VMEM((m_dev, size), bf16),
            pltpu.VMEM((m_dev, size), bf16),
            pltpu.VMEM((m_dev, size), bf16),
            pltpu.VMEM((block_mask.shape[1], size), f32),
            pltpu.VMEM((block_mask.shape[1], size), f32),
            pltpu.VMEM((m_dev, m_dev), bf16),
            dma((n_row + n_col - 2,)), dma((n_row + n_col - 2,)),
            dma((n_col - 1,)), dma((n_col - 1,)),
            dma((n_row - 1,)), dma((n_row - 1,)),
            dma((n_row - 1,)), dma((n_row - 1,)),
            dma((n_col - 1,)), dma((n_col - 1,)),
            dma((n_z,)), dma((n_z,)),
            dma((9,)),
            pltpu.SemaphoreType.REGULAR,
        ],
        compiler_params=pltpu.CompilerParams(
            collective_id=0, has_side_effects=True, vmem_limit_bytes=48 * 1024 * 1024
        ),
    )(
        *[
            pltpu.with_memory_space_constraint(item, pltpu.HBM)
            for item in (
                diag_block,
                pivot_order,
                jnp.swapaxes(lower_in, 1, 2),
                upper_in,
                trailing,
                jnp.swapaxes(block_mask, 1, 2),
                row_map,
            )
        ]
    )
    return merged[None]


def solution(mesh):
    return jax.shard_map(
        local,
        mesh=mesh,
        in_specs=(
            P("cube", ("row", "col"), None),
            P("cube", None),
            P("cube", "row", "col"),
            P("cube", "row", "col"),
            P("cube", "row", "col"),
            P("cube", "row", "col"),
            P("cube", "row"),
        ),
        out_specs=P("cube", "row", "col"),
        check_vma=False,
    )
```

```python
import functools

import jax
import jax.numpy as jnp
from jax import lax
from jax.experimental import pallas as pl
from jax.experimental.pallas import tpu as pltpu
from jax.sharding import PartitionSpec as P

MESH = pl.DeviceIdType.MESH
RAW = (384, 256)
COOKED = (128, 256, 384, 384, 128)
STEP = 64
GROUP = 8


def offsets(widths, start):
    spans = []
    for width in widths:
        spans.append((start, width))
        start += width
    return spans


def invert(amat):
    size = amat.shape[0]
    narrow = 128
    lane = lax.broadcasted_iota(jnp.int32, (1, size), 1)
    sub = lax.broadcasted_iota(jnp.int32, (STEP, 1), 0)

    def block_step(_, carry):
        x = amat[0:STEP, :]
        for first in range(0, STEP, GROUP):
            columns = [
                jnp.broadcast_to(x[:, k : k + 1], (STEP, narrow))
                for k in range(first, first + GROUP)
            ]
            for j in range(GROUP):
                k = first + j
                inverse = 1.0 / columns[j][k : k + 1, :]
                for later in range(j + 1, GROUP):
                    ratio = columns[later][k : k + 1, :] * inverse
                    columns[later] = jnp.where(
                        sub == k, ratio, columns[later] - columns[j] * ratio
                    )
                here = lane == k
                column = jnp.concatenate([columns[j]] * (size // narrow), axis=1)
                inverse = jnp.concatenate([inverse] * (size // narrow), axis=1)
                fresh = jnp.where(here, inverse, x[k : k + 1, :] * inverse)
                x = jnp.where(sub == k, fresh, jnp.where(here, 0.0, x) - column * fresh)
        below = amat[STEP:, :]
        rest = jnp.where(lane < STEP, 0.0, below) - jnp.dot(
            below[:, 0:STEP],
            x,
            precision=lax.Precision.HIGHEST,
            preferred_element_type=jnp.float32,
        )
        amat[0 : size - STEP, :] = jnp.concatenate([rest[:, STEP:], rest[:, :STEP]], axis=1)
        amat[size - STEP :, :] = jnp.concatenate([x[:, STEP:], x[:, :STEP]], axis=1)
        return carry

    lax.fori_loop(0, size // STEP, block_step, 0)


def update(block, spans_from, panel, right, right_from, width):
    rows = 256

    def body(step, carry):
        top = pl.multiple_of(step * rows, rows)
        product = jnp.dot(
            panel[pl.ds(top, rows), :],
            right[:, pl.ds(right_from, width)],
            preferred_element_type=jnp.float32,
        )
        where = (pl.ds(top, rows), pl.ds(spans_from, width))
        block[where] = (block[where].astype(jnp.float32) - product).astype(jnp.bfloat16)
        return carry

    lax.fori_loop(0, block.shape[0] // rows, body, 0)


def kernel(
    diag, order_in, lower, upper, trailing, mask_in, row_map_in, keep,
    order_s, order_v, mask, row_map, dg, lt, u, ug, land, cook, amat, wk, ws, wo, wg, mo, mg, part_sum, perm,
    d_send, d_recv, l_send, l_recv, u_send, u_recv, f_send, f_recv,
    v_send, v_recv, z_send, z_recv, local_sem, gate,
):
    n_row, n_col = lax.axis_size("row"), lax.axis_size("col")
    c, r, q = lax.axis_index("cube"), lax.axis_index("row"), lax.axis_index("col")
    parity = lax.rem(c, 2)
    peer = (c + 1 - 2 * parity, r, q)
    row_mates = [(c, lax.rem(r + d, n_row), q) for d in range(1, n_row)]
    col_mates = [(c, r, lax.rem(q + d, n_col)) for d in range(1, n_col)]

    m_dev = keep.shape[0]
    half = keep.shape[1]
    raw_width = ug.shape[1]
    kept_at = pl.multiple_of(parity * half, 128)
    sent_at = pl.multiple_of((1 - parity) * half, 128)
    raw_spans = offsets(RAW, 0)
    cooked_spans = offsets(COOKED, raw_width)

    def remote(src, dst, send, recv, to):
        return pltpu.make_async_remote_copy(
            src_ref=src, dst_ref=dst, send_sem=send, recv_sem=recv,
            device_id=to, device_id_type=MESH,
        )

    small = []
    for i, (src, dst) in enumerate(
        [(mask_in, mask), (order_in, order_s), (order_in, order_v), (row_map_in, row_map)]
    ):
        copy = pltpu.make_async_copy(src, dst, local_sem.at[5 + i])
        copy.start()
        small.append(copy)

    barrier = pltpu.get_barrier_semaphore()

    def signal(semaphore, to):
        pl.semaphore_signal(semaphore, inc=1, device_id=to, device_id_type=MESH)

    @pl.when(parity == 1)
    def _():
        signal(barrier, peer)

    @pl.when(parity == 0)
    def _():
        pl.semaphore_wait(barrier, 1)
        signal(gate, peer)

    @pl.when(parity == 1)
    def _():
        pl.semaphore_wait(gate, 1)

    d_rows = diag.shape[1]
    d_at = pl.multiple_of(q * d_rows, d_rows)
    u_rows = upper.shape[1]
    u_at = pl.multiple_of(r * u_rows, u_rows)
    l_rows = lower.shape[1]
    l_at = pl.multiple_of(q * l_rows, l_rows)
    w_rows = m_dev // n_col
    w_at = pl.multiple_of(q * w_rows, w_rows)

    z_copies = []

    def to_peer(src, dst):
        i = len(z_copies)
        copy = remote(src, dst, z_send.at[i], z_recv.at[i], peer)
        copy.start()
        z_copies.append(copy)
        return copy

    raw = [
        to_peer(trailing.at[0, :, pl.ds(sent_at + at, width)], land.at[:, pl.ds(at, width)])
        for at, width in raw_spans
    ]
    u_raw = to_peer(
        upper.at[0, :, pl.ds(sent_at, raw_width)], ug.at[pl.ds(u_at, u_rows), :]
    )

    @pl.when(parity == 1)
    def _():
        for mate in row_mates + col_mates:
            signal(barrier, mate)
        pl.semaphore_wait(barrier, n_row + n_col - 2)
        signal(gate, peer)

    @pl.when(parity == 0)
    def _():
        pl.semaphore_wait(gate, 1)

    d_own = pltpu.make_async_copy(diag.at[0], dg.at[r, pl.ds(d_at, d_rows), :], local_sem.at[0])
    d_own.start()
    d_first = []
    for i, mate in enumerate(row_mates):
        copy = remote(diag.at[0], dg.at[r, pl.ds(d_at, d_rows), :], d_send.at[i], d_recv.at[i], mate)
        copy.start()
        d_first.append(copy)

    small[0].wait()
    for i in range(mo.shape[0]):
        flag = mask[0, 1 - parity, i].astype(jnp.float32)
        mo[i : i + 1, :] = jnp.full((1, mo.shape[1]), flag, jnp.float32)
    m_raw = to_peer(mo, mg)

    d_own.wait()
    for copy in d_first:
        copy.wait_recv()
    d_second = []
    for i, mate in enumerate(col_mates):
        part = dg.at[:, pl.ds(d_at, d_rows), :]
        copy = remote(part, part, d_send.at[n_row - 1 + i], d_recv.at[n_row - 1 + i], mate)
        copy.start()
        d_second.append(copy)

    def spread(at, width, turn):
        src = upper.at[0, :, pl.ds(at, width)]
        dst = u.at[pl.ds(u_at, u_rows), pl.ds(at, width)]
        own = pltpu.make_async_copy(src, dst, local_sem.at[2 + 7 * turn])
        own.start()
        away = []
        for i, mate in enumerate(row_mates):
            sem = turn * (n_row - 1) + i
            copy = remote(src, dst, u_send.at[sem], u_recv.at[sem], mate)
            copy.start()
            away.append(copy)
        return own, away

    u_cook = spread(sent_at + raw_width, half - raw_width, 0)
    l_own = pltpu.make_async_copy(lower.at[0], lt.at[pl.ds(l_at, l_rows), :], local_sem.at[1])
    l_own.start()
    l_copies = []
    for i, mate in enumerate(col_mates):
        copy = remote(lower.at[0], lt.at[pl.ds(l_at, l_rows), :], l_send.at[i], l_recv.at[i], mate)
        copy.start()
        l_copies.append(copy)
    u_kept = spread(kept_at, half, 1)
    cook_in = pltpu.make_async_copy(
        trailing.at[0, :, pl.ds(sent_at + raw_width, half - raw_width)], cook, local_sem.at[3]
    )
    cook_in.start()
    keep_in = pltpu.make_async_copy(
        trailing.at[0, :, pl.ds(kept_at, half)], keep, local_sem.at[4]
    )
    keep_in.start()

    for copy in small[1:]:
        copy.wait()
    tile = 128
    lane = lax.broadcasted_iota(jnp.int32, (tile, tile), 1)
    for i in range(m_dev // tile):
        along = jnp.broadcast_to(row_map[:, i * tile : (i + 1) * tile], (tile, tile))
        target = along.astype(jnp.float32).T.astype(jnp.int32)
        for j in range(m_dev // tile):
            hit = jnp.where(lane + j * tile == target, 1.0, 0.0)
            perm[i * tile : (i + 1) * tile, j * tile : (j + 1) * tile] = hit.astype(jnp.bfloat16)

    for copy in d_second:
        copy.wait_recv()
    size = amat.shape[0]
    per_row = dg.shape[1]

    def pick(i, carry):
        source = order_s[0, i]
        amat[pl.ds(i, 1), :] = dg[source // per_row, pl.ds(source % per_row, 1), :]
        return carry

    lax.fori_loop(0, size, pick, 0, unroll=8)
    invert(amat)

    u_raw.wait_recv()
    u_pass = []
    for i, mate in enumerate(row_mates):
        part = ug.at[pl.ds(u_at, u_rows), :]
        copy = remote(part, part, f_send.at[i], f_recv.at[i], mate)
        copy.start()
        u_pass.append(copy)

    xt = amat[...].T
    high = xt.astype(jnp.bfloat16)
    left = xt - high.astype(jnp.float32)
    middle = left.astype(jnp.bfloat16)
    low = (left - middle.astype(jnp.float32)).astype(jnp.bfloat16)
    subs = lax.broadcasted_iota(jnp.int32, (size, size), 0)
    hot = jnp.where(subs == order_v[...], 1.0, 0.0).astype(jnp.bfloat16)
    high, middle, low = [
        jnp.dot(hot, part, preferred_element_type=jnp.float32).astype(jnp.bfloat16)
        for part in (high, middle, low)
    ]
    l_own.wait()
    for copy in l_copies:
        copy.wait_recv()
    wide = 256

    def panel(i, carry):
        part = lt[:, pl.ds(pl.multiple_of(i * wide, wide), wide)]
        wt = (
            jnp.dot(low, part, preferred_element_type=jnp.float32)
            + jnp.dot(middle, part, preferred_element_type=jnp.float32)
            + jnp.dot(high, part, preferred_element_type=jnp.float32)
        )
        w = wt.T
        for j in range(wide // tile):
            at = pl.multiple_of(i * wide + j * tile, tile)
            rows = w[j * tile : (j + 1) * tile, :]
            flag = mask[0, 1 - parity, i * (wide // tile) + j].astype(jnp.float32)
            ws[pl.ds(at, tile), :] = (rows * flag).astype(jnp.bfloat16)
            wo[pl.ds(at, tile), :] = rows.astype(jnp.bfloat16)
        return carry

    lax.fori_loop(0, m_dev // wide, panel, 0)
    w_raw = to_peer(wo.at[pl.ds(w_at, w_rows), :], wg.at[pl.ds(w_at, w_rows), :])

    u_cook[0].wait()
    for copy in u_cook[1]:
        copy.wait_recv()
    cook_in.wait()
    cooked = []
    for at, width in cooked_spans:
        start = at - raw_width
        update(cook, start, ws, u, sent_at + at, width)
        if at + width < half:
            cooked.append(to_peer(cook.at[:, pl.ds(start, width)], land.at[:, pl.ds(at, width)]))
    last_at, last = cooked_spans[-1]
    upper_half = m_dev // 2
    tail = [
        to_peer(
            cook.at[pl.ds(top, upper_half), pl.ds(last_at - raw_width, last)],
            land.at[pl.ds(top, upper_half), pl.ds(last_at, last)],
        )
        for top in (0, upper_half)
    ]

    for i in range(m_dev // tile):
        block = slice(i * tile, (i + 1) * tile)
        flag = mask[0, parity, i].astype(jnp.float32)
        wk[block, :] = (wo[block, :].astype(jnp.float32) * flag).astype(jnp.bfloat16)
    keep_in.wait()
    u_kept[0].wait()
    for copy in u_kept[1]:
        copy.wait_recv()
    for at in range(0, half, 384):
        update(keep, at, wk, u, kept_at + at, 384)

    w_raw.wait_recv()
    w_pass = []
    for i, mate in enumerate(col_mates):
        part = wg.at[pl.ds(w_at, w_rows), :]
        copy = remote(part, part, v_send.at[i], v_recv.at[i], mate)
        copy.start()
        w_pass.append(copy)
    for copy in [m_raw] + u_pass + w_pass:
        copy.wait_recv()
    for i in range(mg.shape[0]):
        block = slice(i * tile, (i + 1) * tile)
        flag = jnp.concatenate([mg[i : i + 1, :]] * (size // tile), axis=1)
        masked = wg[block, :].astype(jnp.float32) * flag
        ws[block, :] = masked.astype(jnp.bfloat16)

    def merge(at, width):
        rows = 512 if width <= tile else 256

        def body(step, carry):
            top = pl.multiple_of(step * rows, rows)
            taken = jnp.dot(
                perm[pl.ds(top, rows), :],
                land[:, at : at + width],
                preferred_element_type=jnp.float32,
            )
            where = (pl.ds(top, rows), pl.ds(at, width))
            keep[where] = (keep[where].astype(jnp.float32) + taken).astype(jnp.bfloat16)
            return carry

        lax.fori_loop(0, m_dev // rows, body, 0)

    for (at, width), copy in zip(raw_spans, raw):
        copy.wait_recv()
        update(land, at, ws, ug, at, width)
        merge(at, width)
    for (at, width), copy in zip(cooked_spans, cooked):
        copy.wait_recv()
        merge(at, width)

    tail[0].wait_recv()
    for top in range(0, m_dev, upper_half):
        rows = slice(top, top + upper_half)
        part_sum[rows, :] = jnp.dot(
            perm[rows, :upper_half],
            land[:upper_half, last_at:],
            preferred_element_type=jnp.float32,
        )
    tail[1].wait_recv()
    for top in range(0, m_dev, upper_half):
        rows = slice(top, top + upper_half)
        taken = part_sum[rows, :] + jnp.dot(
            perm[rows, upper_half:],
            land[upper_half:, last_at:],
            preferred_element_type=jnp.float32,
        )
        total = keep[rows, last_at:].astype(jnp.float32) + taken
        keep[rows, last_at:] = total.astype(jnp.bfloat16)

    for copy in d_first + d_second + l_copies + u_cook[1] + u_kept[1] + u_pass + w_pass + z_copies:
        copy.wait_send()


def local(diag_block, pivot_order, lower_in, upper_in, trailing, block_mask, row_map):
    n_row, n_col = lax.axis_size("row"), lax.axis_size("col")
    size = diag_block.shape[2]
    m_dev, wide = trailing.shape[1:]
    half = wide // 2
    raw_width = sum(RAW)
    n_z = 4 + len(RAW) + len(COOKED)
    dma = pltpu.SemaphoreType.DMA
    bf16, f32 = jnp.bfloat16, jnp.float32
    hbm = pl.BlockSpec(memory_space=pltpu.HBM)
    merged = pl.pallas_call(
        kernel,
        out_shape=jax.ShapeDtypeStruct((m_dev, half), bf16),
        in_specs=[hbm] * 7,
        out_specs=pl.BlockSpec(memory_space=pltpu.VMEM),
        scratch_shapes=[
            pltpu.SMEM(pivot_order.shape, jnp.int32),
            pltpu.VMEM(pivot_order.shape, jnp.int32),
            pltpu.SMEM((1, block_mask.shape[2], block_mask.shape[1]), jnp.int32),
            pltpu.VMEM(row_map.shape, jnp.int32),
            pltpu.VMEM((n_row, size // n_row, size), f32),
            pltpu.VMEM((size, m_dev), bf16),
            pltpu.VMEM((size, wide), bf16),
            pltpu.VMEM((size, raw_width), bf16),
            pltpu.VMEM((m_dev, half), bf16),
            pltpu.VMEM((m_dev, half - raw_width), bf16),
            pltpu.VMEM((size, size), f32),
            pltpu.VMEM((m_dev, size), bf16),
            pltpu.VMEM((m_dev, size), bf16),
            pltpu.VMEM((m_dev, size), bf16),
            pltpu.VMEM((m_dev, size), bf16),
            pltpu.VMEM((block_mask.shape[1], 128), f32),
            pltpu.VMEM((block_mask.shape[1], 128), f32),
            pltpu.VMEM((m_dev, 128), f32),
            pltpu.VMEM((m_dev, m_dev), bf16),
            dma((n_row + n_col - 2,)), dma((n_row + n_col - 2,)),
            dma((n_col - 1,)), dma((n_col - 1,)),
            dma((2 * n_row - 2,)), dma((2 * n_row - 2,)),
            dma((n_row - 1,)), dma((n_row - 1,)),
            dma((n_col - 1,)), dma((n_col - 1,)),
            dma((n_z,)), dma((n_z,)),
            dma((10,)),
            pltpu.SemaphoreType.REGULAR,
        ],
        compiler_params=pltpu.CompilerParams(
            collective_id=0, has_side_effects=True, vmem_limit_bytes=48 * 1024 * 1024
        ),
    )(
        *[
            pltpu.with_memory_space_constraint(item, pltpu.HBM)
            for item in (
                diag_block,
                pivot_order,
                jnp.swapaxes(lower_in, 1, 2),
                upper_in,
                trailing,
                jnp.swapaxes(block_mask, 1, 2),
                row_map,
            )
        ]
    )
    return merged[None]


def solution(mesh):
    return jax.shard_map(
        local,
        mesh=mesh,
        in_specs=(
            P("cube", ("row", "col"), None),
            P("cube", None),
            P("cube", "row", "col"),
            P("cube", "row", "col"),
            P("cube", "row", "col"),
            P("cube", "row", "col"),
            P("cube", "row"),
        ),
        out_specs=P("cube", "row", "col"),
        check_vma=False,
    )
```
